32 devices in a mesh: row: 16 (over z, x, core), col: 2 (over y).
Axes of the slice: x: 2, y: 2, z: 4, core: 2. Of those that a mesh axis runs over, the one named last changes fastest.
Arguments:
- object_field: float32 [2, 2, 2048, 256], P(None, None, 'row', 'col'), may hold values from -1 to 1
- probe: float32 [4, 2, 128, 128], replicated, may hold values from -3 to 3
- kernel_phase: float32 [128, 128], replicated, may hold values from -3.140625 to 3.140625
- amplitudes: float32 [3, 16, 2, 128, 128], P(None, 'row', 'col'), may hold values from 0.05 to 1
- offsets: int32 [3, 16, 2, 2], P(None, 'row', 'col'), may hold values from 0 to 64
Outputs:
- object_out: float32 [2, 2, 2048, 256], P(None, None, 'row', 'col')
- probe_out: float32 [4, 2, 128, 128], replicated
The draws below stay inside these ranges and needn't reach their ends.
Inputs may be any that keep to these rules, and one draw needn't show every extreme that they name: offsets[b, r + p, c] place a window of 128 x 128 pixels inside tile (r, c) extended by 32 pixels on each side.
All inputs are finite; a program needn't handle non-finite values.
Results may differ from the reference program's by a relative error of at most 0.0003.
Values sent between devices are 32-bit elements; how exact they have to be, the bound alone decides.
A program may use at most 128 MiB of HBM per device.

```python
import math
import jax
import jax.numpy as jnp
from jax import lax

TILE = 128
WIN = 128
OVL = 32
MODES = 4
SLICES = 2
BATCHES = 3
NPOS = 1
OBJ_ROWS = 2048
OBJ_COLS = 256
POS_ROWS = 16
N_ROW = 16
N_COL = 2


def plant(values, stream_key, least, top_value):
    shape = values.shape
    index_at = [jax.random.randint(jax.random.fold_in(stream_key, axis), (), 0, shape[axis]) for axis in range(len(shape))]
    values = values.at[tuple(index_at)].set(least)
    longest = shape.index(max(shape))
    index_at[longest] = (index_at[longest] + 1) % shape[longest]
    return values.at[tuple(index_at)].set(top_value)


def block_levels(own_key, extent, shards, smallest, largest):
    def one(axis_at, parts):
        heights = jax.random.uniform(jax.random.fold_in(jax.random.fold_in(own_key, 6), axis_at), (parts,), jnp.float32, smallest / len(shards), largest / len(shards))
        return jnp.repeat(jnp.exp(heights), extent[axis_at] // parts).reshape((-1,) + (1,) * (len(extent) - axis_at - 1))

    factor_of = one(*shards[0])
    for cut in shards[1:]:
        factor_of = factor_of * one(*cut)
    return factor_of


def scatter_about(rng, extent, deviation, bound, held_as=jnp.bfloat16):
    return jnp.clip(deviation * jax.random.normal(rng, extent, jnp.float32), -bound, bound).astype(held_as)


def setup_inputs(seed: int = 0) -> dict:
    key_of = jax.random.split(jax.random.key(seed), 6)
    return {
        "object_field": jnp.clip(jax.random.uniform(key_of[0], (SLICES, 2, OBJ_ROWS, OBJ_COLS), jnp.float32, -1.0, 1.0) * block_levels(key_of[0], (SLICES, 2, OBJ_ROWS, OBJ_COLS), ((2, 16), (3, 2)), -0.4, 0.0), -1.0, 1.0),
        "probe": scatter_about(key_of[1], (MODES, 2, WIN, WIN), 0.5, 3.0, jnp.float32),
        "kernel_phase": jnp.clip(jax.random.uniform(key_of[2], (WIN, WIN), jnp.float32, -3.140625, 3.140625), -3.140625, 3.140625),
        "amplitudes": jnp.clip(jnp.exp(math.log(1.0) - 2.9957323 * jax.random.uniform(key_of[3], (BATCHES, POS_ROWS, N_COL, WIN, WIN), jnp.float32) ** block_levels(key_of[3], (BATCHES, POS_ROWS, N_COL, WIN, WIN), ((1, 16), (2, 2)), -0.2, 0.2)), 0.05, 1.0),
        "offsets": plant(jax.random.randint(key_of[4], (BATCHES, POS_ROWS, N_COL, 2), 0, 2 * OVL + 1), jax.random.fold_in(key_of[4], 1), 0, 2 * OVL).astype(jnp.int32),
    }


OBJECT_RATE = 0.5
PROBE_RATE = 0.5
FLOOR = 0.1

def spread_wave(field, kernel):
    return jnp.fft.ifft2(jnp.fft.fft2(field, norm='ortho') * kernel, norm='ortho')

def window_gradients(object_window, probe_wave, kernel, measured):
    first_slice = object_window[0, 0] + 1j * object_window[0, 1]
    second_slice = object_window[1, 0] + 1j * object_window[1, 1]
    entrance = probe_wave * first_slice
    spread = spread_wave(entrance, kernel)
    exit_wave = spread * second_slice
    farfield = jnp.fft.fft2(exit_wave, norm='ortho')
    intensity = lax.optimization_barrier(jnp.sum(jnp.real(farfield) ** 2 + jnp.imag(farfield) ** 2, axis=0))
    factor = 1.0 - measured / jnp.sqrt(intensity + FLOOR)
    back_second = jnp.fft.ifft2(farfield * factor, norm='ortho')
    grad_second = lax.optimization_barrier(jnp.sum(jnp.conj(spread) * back_second, axis=0))
    back_first = spread_wave(jnp.conj(second_slice) * back_second, jnp.conj(kernel))
    grad_first = lax.optimization_barrier(jnp.sum(jnp.conj(probe_wave) * back_first, axis=0))
    grad_probe = jnp.conj(first_slice) * back_first
    object_grad = jnp.stack([jnp.stack([jnp.real(grad_first), jnp.imag(grad_first)]), jnp.stack([jnp.real(grad_second), jnp.imag(grad_second)])])
    probe_grad = jnp.stack([jnp.real(grad_probe), jnp.imag(grad_probe)], axis=1)
    return (object_grad, probe_grad)

def reference(object_field, probe, kernel_phase, amplitudes, offsets):
    kernel = jnp.cos(kernel_phase) + 1j * jnp.sin(kernel_phase)
    probe_rate = PROBE_RATE / math.sqrt(N_ROW * N_COL * NPOS)
    windows_total = N_ROW * N_COL * NPOS
    current = object_field
    probe_now = probe
    pending = jnp.zeros_like(probe)
    for batch_index in range(BATCHES):
        padded = jnp.pad(current, ((0, 0), (0, 0), (OVL, OVL), (OVL, OVL)))
        probe_wave = probe_now[:, 0] + 1j * probe_now[:, 1]

        def visit(carry, window_index):
            object_sum, probe_sum = carry
            slot_index = window_index // N_COL
            column_index = window_index % N_COL
            tile_row = slot_index // NPOS
            offset_pair = offsets[batch_index, slot_index, column_index]
            top_row = (tile_row * TILE + offset_pair[0]).astype(jnp.int32)
            left_col = (column_index * TILE + offset_pair[1]).astype(jnp.int32)
            anchor = jnp.zeros((), jnp.int32)
            starts = (anchor, anchor, top_row, left_col)
            window_shape = (SLICES, 2, WIN, WIN)
            object_window = lax.dynamic_slice(padded, starts, window_shape)
            measured = amplitudes[batch_index, slot_index, column_index]
            object_grad, probe_grad = window_gradients(object_window, probe_wave, kernel, measured)
            previous = lax.dynamic_slice(object_sum, starts, window_shape)
            object_sum = lax.dynamic_update_slice(object_sum, previous + object_grad, starts)
            return ((object_sum, probe_sum + probe_grad), None)
        initial = (jnp.zeros_like(padded), jnp.zeros_like(probe))
        (object_sum, probe_sum), unused = lax.scan(visit, initial, jnp.arange(windows_total, dtype=jnp.int32))
        current = current - OBJECT_RATE * object_sum[:, :, OVL:OVL + TILE * N_ROW, OVL:OVL + TILE * N_COL]
        probe_now = probe_now - probe_rate * pending
        pending = probe_sum
    probe_now = probe_now - probe_rate * pending
    return (current, probe_now)
```

```python
import functools
import math

import jax
import jax.numpy as jnp
import numpy as np
from jax import lax
from jax.experimental import pallas as pl
from jax.experimental.pallas import tpu as pltpu
from jax.sharding import PartitionSpec as P

OVL = 32
OBJECT_RATE = 0.5
PROBE_RATE = 0.5
FLOOR = 0.1
MESH = pl.DeviceIdType.MESH
F32 = jnp.float32
BF16 = jnp.bfloat16

SIDES = ((-1, 0), (1, 0), (0, -1), (0, 1), (-1, -1), (-1, 1), (1, -1), (1, 1))


def split(values):
    high = values.astype(BF16)
    return high, (values - high.astype(F32)).astype(BF16)


def dft_matrices(window):
    counter = np.arange(window)
    phases = (counter[:, None] * counter[None, :] % window) * (-2.0 * np.pi / window)
    c, s = np.cos(phases) / math.sqrt(window), np.sin(phases) / math.sqrt(window)
    left = np.block([[c, -s], [s, c]]).astype(np.float32)
    out = []
    for m in (left, left.T):
        high = m.astype(BF16)
        out += [high, (m - high.astype(np.float32)).astype(BF16)]
    return np.stack(out)


def dot(a, b):
    return jnp.dot(a, b, preferred_element_type=F32)


def product(a, b):
    return dot(a[0], b[0]) + (dot(a[0], b[1]) + dot(a[1], b[0]))


def dft(fields, tables, inverse):
    first, second = (tables[1], tables[0]) if inverse else tables
    w = fields[0][0].shape[0]
    x = jnp.concatenate(
        [jnp.concatenate([f[k] for f in fields], axis=1) for k in range(2)], axis=0
    )
    y = product(first, split(x))
    z = jnp.concatenate(
        [
            jnp.concatenate([y[:w, m * w : m * w + w], y[w:, m * w : m * w + w]], axis=1)
            for m in range(len(fields))
        ],
        axis=0,
    )
    r = product(split(z), second)
    return [(r[m * w : m * w + w, :w], r[m * w : m * w + w, w:]) for m in range(len(fields))]


def cmul(a, b):
    return a[0] * b[0] - a[1] * b[1], a[0] * b[1] + a[1] * b[0]


def conj_mul(a, b):
    return a[0] * b[0] + a[1] * b[1], a[0] * b[1] - a[1] * b[0]


def csum(pairs):
    re, im = pairs[0]
    for p in pairs[1:]:
        re, im = re + p[0], im + p[1]
    return re, im


def stages_of(rows, n_row, n_col):
    out = []
    for group, n in (("core", 2), ("col", n_col), ("rest", n_row // 2)):
        if n < 2:
            continue
        scatter = rows % (8 * n) == 0
        rows = rows // n if scatter else rows
        out.append((group, n, scatter, rows))
    return out


def kernel(
    n_row, n_col, batches, modes, stages,
    off_ref, obj_ref, probe_ref, phase_ref, amp_ref, tab_ref,
    obj_out, probe_out,
    ext, ziel, grad, strip, from_row, from_col, from_corner,
    phi_ref, kern_ref, pnow, acc, gat, *rest,
):
    stage_bufs = rest[: len(stages)]
    ex_send, ex_recv, rs_send, rs_recv, ag_send, ag_recv = rest[len(stages) :]
    w = obj_ref.shape[-1]
    full = w + 2 * OVL
    band = 2 * OVL
    row, col = lax.axis_index("row"), lax.axis_index("col")

    def there(dr, dc):
        ok = None
        if dr:
            ok = row > 0 if dr < 0 else row < n_row - 1
        if dc:
            c = col > 0 if dc < 0 else col < n_col - 1
            ok = c if ok is None else jnp.logical_and(ok, c)
        return ok

    def member(group, d):
        if group == "core":
            return row + 1 - 2 * lax.rem(row, 2), col
        if group == "col":
            return row, lax.rem(col + d, n_col)
        n = n_row // 2
        return 2 * lax.rem(lax.div(row, 2) + d, n) + lax.rem(row, 2), col

    def rank(group):
        if group == "core":
            return lax.rem(row, 2)
        return col if group == "col" else lax.div(row, 2)

    barrier = pltpu.get_barrier_semaphore()
    expected = 0
    for dr, dc in SIDES:
        ok = there(dr, dc)
        expected = expected + ok.astype(jnp.int32)

        @pl.when(ok)
        def _():
            pl.semaphore_signal(
                barrier, inc=1, device_id=(row + dr, col + dc), device_id_type=MESH
            )

    for group, n, _, _ in stages:
        for d in range(1, n):
            pl.semaphore_signal(barrier, inc=1, device_id=member(group, d), device_id_type=MESH)
        expected = expected + (n - 1)

    lane = lax.broadcasted_iota(jnp.int32, (full, w), 1)
    line = lax.broadcasted_iota(jnp.int32, (full, w), 0)
    low, high = lane < OVL, lane >= w - OVL
    left_part = high | ((lane >= OVL) & (lane < 2 * OVL))
    top, bottom = row == 0, row == n_row - 1
    row_ok = (jnp.logical_not(top) | (line >= OVL)) & (jnp.logical_not(bottom) | (line < w + OVL))
    at_left, at_right = col == 0, col == n_col - 1
    col_ok = (left_part & jnp.logical_not(at_left)) | (
        jnp.logical_not(left_part) & jnp.logical_not(at_right)
    )
    side_ok = row_ok & col_ok

    def swap(x):
        return pltpu.roll(x, w // 2, x.ndim - 1)

    def send(e):
        for p in range(2):
            side, a, b = grad[e, 4 + p], grad[e, 2 * p], swap(grad[e, 2 * p + 1])
            strip[e, 0, p] = jnp.where(left_part, side, jnp.where(low, a, b))
            strip[e, 1, p] = jnp.where(left_part, jnp.where(high, a, b), side)
        for k in range(8):
            dr, dc = SIDES[k]

            @pl.when(there(dr, dc))
            def _():
                copy_of(e, k).start()

    def copy_of(e, k):
        dr, dc = SIDES[k]
        rows = pl.ds(0 if dr < 0 else w, band)
        if dc == 0:
            src, dst = grad.at[e, :, rows], from_row.at[e, k]
        elif dr == 0:
            src, dst = strip.at[e, k - 2], from_col.at[e, k - 2]
        else:
            src, dst = strip.at[e, 0 if dc < 0 else 1, :, rows], from_corner.at[e, k - 4]
        return pltpu.make_async_remote_copy(
            src_ref=src, dst_ref=dst, send_sem=ex_send.at[e, k], recv_sem=ex_recv.at[e, k],
            device_id=(row + dr, col + dc), device_id_type=MESH,
        )

    def receive(e, scale):
        for f in range(6):
            ext[f] = ext[f] + scale * grad[e, f] if e else grad[e, f]
        for k in range(8):
            dr, dc = SIDES[k]

            @pl.when(there(-dr, -dc))
            def _():
                copy_of(e, k).wait_recv()
                rows = pl.ds(w if dr < 0 else 0, band)
                if dc == 0:
                    for f in range(6):
                        ext[f, rows] = ext[f, rows] + scale * from_row[e, k, f]
                    return
                if dr == 0:
                    rows = pl.ds(0, full)
                count = full if dr == 0 else band
                lp, lo, hi = left_part[:count], low[:count], high[:count]
                for p in range(2):
                    x = from_col[e, k - 2, p] if dr == 0 else from_corner[e, k - 4, p]
                    x = scale * x
                    y = swap(x)
                    edge, mine = (lo, lp) if dc > 0 else (hi, jnp.logical_not(lp))
                    ext[4 + p, rows] = ext[4 + p, rows] + jnp.where(mine, x, 0.0)
                    ext[2 * p, rows] = ext[2 * p, rows] + jnp.where(edge, x, 0.0)
                    ext[2 * p + 1, rows] = ext[2 * p + 1, rows] + jnp.where(edge, y, 0.0)

    def sent(e):
        for k in range(8):
            dr, dc = SIDES[k]

            @pl.when(there(dr, dc))
            def _():
                copy_of(e, k).wait_send()

    def base_of(s):
        rows = acc.shape[1]
        base = 0
        for group, n, scatter, after in stages[:s]:
            if scatter:
                base = base + rank(group) * after
        return base

    def rs_copies(q, s):
        group, n, scatter, after = stages[s]
        base, mine = base_of(s), rank(group)
        for d in range(1, n):
            to = lax.rem(mine + d, n)
            start = pl.multiple_of(base + (to * after if scatter else 0), 8)
            slot = d - 1 if scatter else mine
            yield pltpu.make_async_remote_copy(
                src_ref=acc.at[q, pl.ds(start, after)], dst_ref=stage_bufs[s].at[q, slot],
                send_sem=rs_send.at[q, s, d], recv_sem=rs_recv.at[q, s, d],
                device_id=member(group, d), device_id_type=MESH,
            )

    def rs_start(q, s):
        for c in rs_copies(q, s):
            c.start()

    def rs_end(q, s):
        group, n, scatter, after = stages[s]
        start = pl.multiple_of(base_of(s + 1), 8)
        place = pl.ds(start, after)
        buf = stage_bufs[s]
        if not scatter:
            buf[q, rank(group)] = acc[q, place]
        for c in rs_copies(q, s):
            c.wait()
        total = acc[q, place] if scatter else buf[q, 0]
        for j in range(0 if scatter else 1, n - 1 if scatter else n):
            total = total + buf[q, j]
        if s == len(stages) - 1:
            gat[q, place] = total
        else:
            acc[q, place] = total

    def ag_copies(q, s):
        group, n, scatter, after = stages[s]
        place = pl.ds(pl.multiple_of(base_of(s + 1), 8), after)
        for d in range(1, n if scatter else 1):
            yield pltpu.make_async_remote_copy(
                src_ref=gat.at[q, place], dst_ref=gat.at[q, place],
                send_sem=ag_send.at[q, s, d], recv_sem=ag_recv.at[q, s, d],
                device_id=member(group, d), device_id_type=MESH,
            )

    def ag_start(q, s):
        for c in ag_copies(q, s):
            c.start()

    def ag_end(q, s):
        for c in ag_copies(q, s):
            c.wait()

    def sum_steps(q):
        steps = []
        last = len(stages) - 1
        for s in range(last + 1):
            steps.append((lambda s=s: rs_start(q, s), lambda s=s: rs_end(q, s)))
        for s in range(last, -1, -1):
            steps.append((lambda s=s: ag_start(q, s), lambda s=s: ag_end(q, s)))
        return steps

    running = []

    def advance():
        if running:
            running.pop(0)[1]()
            if running:
                running[0][0]()

    for f in range(6):
        grad[0, f] = jnp.zeros((full, w), F32)
    for f in range(4):
        grad[0, f, OVL : OVL + w] = obj_ref[f]
    pl.semaphore_wait(barrier, expected)
    send(0)
    kern_ref[0] = jnp.cos(phase_ref[...])
    kern_ref[1] = jnp.sin(phase_ref[...])
    ziel[...] = jnp.zeros_like(ziel)
    receive(0, 1.0)

    rate = PROBE_RATE / math.sqrt(n_row * n_col)
    kern = (kern_ref[0], kern_ref[1])
    conj_kern = (kern[0], -kern[1])
    tables = ((tab_ref[0], tab_ref[1]), (tab_ref[2], tab_ref[3]))
    lane_w = lax.broadcasted_iota(jnp.int32, (w, w), 1)

    for b in range(batches):
        if b == 0 or b == 1:
            source = probe_ref
        else:
            while running:
                advance()
            previous = probe_ref if b == 2 else pnow
            for m in range(modes):
                for k in range(2):
                    at = (m * 2 + k) * w
                    pnow[m, k] = previous[m, k] - rate * gat[b - 2, at : at + w]
            source = pnow
        y0, x0 = off_ref[b, 0], off_ref[b, 1]
        start = x0 - OVL
        back = lax.rem(w - start, w)
        back_half = lax.rem(w + w // 2 - start, w)
        inside = (lane_w + start >= 0) & (lane_w + start < w)

        def window(f):
            main = ext[f, pl.ds(y0, w), :]
            side = ext[4 + f // 2, pl.ds(y0, w), :]
            return jnp.where(
                inside,
                pltpu.roll(main, back, 1),
                pltpu.roll(side, back_half if f % 2 else back, 1),
            )

        o1, o2 = (window(0), window(1)), (window(2), window(3))
        probe = [(source[m, 0], source[m, 1]) for m in range(modes)]
        spectrum = dft([cmul(p, o1) for p in probe], tables, False)
        phi = dft([cmul(v, kern) for v in spectrum], tables, True)
        for m in range(modes):
            phi_ref[m, 0], phi_ref[m, 1] = phi[m]
        advance()
        far = dft([cmul(v, o2) for v in phi], tables, False)
        intensity = far[0][0] * far[0][0] + far[0][1] * far[0][1]
        for v in far[1:]:
            intensity = intensity + (v[0] * v[0] + v[1] * v[1])
        factor = 1.0 - amp_ref[b] / jnp.sqrt(intensity + FLOOR)
        chi2 = dft([(v[0] * factor, v[1] * factor) for v in far], tables, True)
        advance()
        g2 = csum([conj_mul((phi_ref[m, 0], phi_ref[m, 1]), chi2[m]) for m in range(modes)])
        spectrum = dft([conj_mul(o2, v) for v in chi2], tables, False)
        chi1 = dft([cmul(v, conj_kern) for v in spectrum], tables, True)
        advance()
        probe = [(source[m, 0], source[m, 1]) for m in range(modes)]
        g1 = csum([conj_mul(probe[m], chi1[m]) for m in range(modes)])
        for f, g in enumerate((*g1, *g2)):
            ziel[f, 2 * OVL : 2 * OVL + w] = g
        ahead = lax.rem(w + start, w)
        outside = (lane - start < 0) | (lane - start >= w)
        others = []
        for f in range(4):
            moved = pltpu.roll(ziel[f, pl.ds(2 * OVL - y0, full), :], ahead, 1)
            grad[b + 1, f] = jnp.where(row_ok & jnp.logical_not(outside), moved, 0.0)
            others.append(jnp.where(outside, moved, 0.0))
        for p in range(2):
            grad[b + 1, 4 + p] = jnp.where(
                side_ok, others[2 * p] + swap(others[2 * p + 1]), 0.0
            )
        send(b + 1)
        advance()
        q = min(b, max(batches - 2, 0))
        for m in range(modes):
            g = conj_mul(o1, chi1[m])
            for k in range(2):
                at = pl.ds((m * 2 + k) * w, w)
                acc[q, at] = g[k] if b == q else acc[q, at] + g[k]
        if b != batches - 2 or batches == 1:
            while running:
                advance()
            running.extend(sum_steps(q))
            running[0][0]()
        receive(b + 1, -OBJECT_RATE)
        if b < batches - 1:
            advance()
        if b == batches - 1:
            for f in range(4):
                obj_out[f] = ext[f, OVL : OVL + w]

    while running:
        advance()
    q = max(batches - 2, 0)
    last = pnow if batches > 2 else probe_ref
    for m in range(modes):
        for k in range(2):
            at = (m * 2 + k) * w
            probe_out[m, k] = last[m, k] - rate * gat[q, at : at + w]
    for e in range(batches + 1):
        sent(e)


def per_device(n_row, n_col, object_field, probe, kernel_phase, amplitudes, offsets):
    batches = amplitudes.shape[0]
    modes, _, w, _ = probe.shape
    full = w + 2 * OVL
    rows = modes * 2 * w
    stages = stages_of(rows, n_row, n_col)
    sums = max(batches - 1, 1)
    most = max(n for _, n, _, _ in stages)
    vmem, smem = pltpu.VMEM, pltpu.SMEM
    dma = pltpu.SemaphoreType.DMA
    scratch = [
        vmem((6, full, w), F32),
        vmem((4, full + 2 * OVL, w), F32),
        vmem((batches + 1, 6, full, w), F32),
        vmem((batches + 1, 2, 2, full, w), F32),
        vmem((batches + 1, 2, 6, 2 * OVL, w), F32),
        vmem((batches + 1, 2, 2, full, w), F32),
        vmem((batches + 1, 4, 2, 2 * OVL, w), F32),
        vmem((modes, 2, w, w), F32),
        vmem((2, w, w), F32),
        vmem((modes, 2, w, w), F32),
        vmem((sums, rows, w), F32),
        vmem((sums, rows, w), F32),
    ]
    for _, n, scatter, after in stages:
        scratch.append(vmem((sums, n - 1 if scatter else n, after, w), F32))
    scratch += [dma((batches + 1, 8))] * 2 + [dma((sums, len(stages), most))] * 4
    whole = pl.BlockSpec(memory_space=vmem)
    obj, new_probe = pl.pallas_call(
        functools.partial(kernel, n_row, n_col, batches, modes, stages),
        out_shape=(
            jax.ShapeDtypeStruct((4, w, w), F32),
            jax.ShapeDtypeStruct(probe.shape, F32),
        ),
        in_specs=[pl.BlockSpec(memory_space=smem)] + [whole] * 5,
        out_specs=(whole, whole),
        scratch_shapes=scratch,
        compiler_params=pltpu.CompilerParams(
            collective_id=0, has_side_effects=True, vmem_limit_bytes=48 * 2**20
        ),
    )(
        offsets.reshape(batches, 2),
        object_field.reshape(4, w, w),
        probe,
        kernel_phase,
        amplitudes.reshape(batches, w, w),
        jnp.asarray(dft_matrices(w)),
    )
    return obj.reshape(object_field.shape), new_probe


def solution(mesh):
    in_specs = (
        P(None, None, "row", "col"),
        P(),
        P(),
        P(None, "row", "col", None, None),
        P(None, "row", "col", None),
    )
    out_specs = (P(None, None, "row", "col"), P())
    return jax.shard_map(
        functools.partial(per_device, mesh.shape["row"], mesh.shape["col"]),
        mesh=mesh, in_specs=in_specs, out_specs=out_specs, check_vma=False,
    )
```

```python
import functools
import math

import jax
import jax.numpy as jnp
import numpy as np
from jax import lax
from jax.experimental import pallas as pl
from jax.experimental.pallas import tpu as pltpu
from jax.sharding import PartitionSpec as P

OVL = 32
OBJECT_RATE = 0.5
PROBE_RATE = 0.5
FLOOR = 0.1
MESH = pl.DeviceIdType.MESH
F32 = jnp.float32
BF16 = jnp.bfloat16

SIDES = ((-1, 0), (1, 0), (0, -1), (0, 1), (-1, -1), (-1, 1), (1, -1), (1, 1))


def split(values):
    high = values.astype(BF16)
    return high, (values - high.astype(F32)).astype(BF16)


def dft_matrices(window):
    counter = np.arange(window)
    phases = (counter[:, None] * counter[None, :] % window) * (-2.0 * np.pi / window)
    c, s = np.cos(phases) / math.sqrt(window), np.sin(phases) / math.sqrt(window)
    left = np.block([[c, -s], [s, c]]).astype(np.float32)
    out = []
    for m in (left, left.T):
        high = m.astype(BF16)
        out += [high, (m - high.astype(np.float32)).astype(BF16)]
    return np.stack(out)


def dot(a, b):
    return jnp.dot(a, b, preferred_element_type=F32)


def product(a, b):
    return dot(a[0], b[0]) + (dot(a[0], b[1]) + dot(a[1], b[0]))


def dft(fields, tables, inverse):
    first, second = (tables[1], tables[0]) if inverse else tables
    w = fields[0][0].shape[0]
    x = jnp.concatenate(
        [jnp.concatenate([f[k] for f in fields], axis=1) for k in range(2)], axis=0
    )
    y = product(first, split(x))
    z = jnp.concatenate(
        [
            jnp.concatenate([y[:w, m * w : m * w + w], y[w:, m * w : m * w + w]], axis=1)
            for m in range(len(fields))
        ],
        axis=0,
    )
    r = product(split(z), second)
    return [(r[m * w : m * w + w, :w], r[m * w : m * w + w, w:]) for m in range(len(fields))]


def cmul(a, b):
    return a[0] * b[0] - a[1] * b[1], a[0] * b[1] + a[1] * b[0]


def conj_mul(a, b):
    return a[0] * b[0] + a[1] * b[1], a[0] * b[1] - a[1] * b[0]


def csum(pairs):
    re, im = pairs[0]
    for p in pairs[1:]:
        re, im = re + p[0], im + p[1]
    return re, im


def stages_of(rows, n_row, n_col):
    out = []
    for group, n in (("core", 2), ("col", n_col), ("rest", n_row // 2)):
        if n < 2:
            continue
        scatter = rows % (8 * n) == 0
        rows = rows // n if scatter else rows
        out.append((group, n, scatter, rows))
    return out


def kernel(
    n_row, n_col, batches, modes, stages,
    off_ref, obj_hbm, probe_hbm, phase_hbm, amp_hbm, tab_hbm,
    obj_out, probe_out,
    ext, ziel, grad, strip, from_row, from_col, from_corner,
    phi_ref, kern_ref, pnow, acc, gat, probe_ref, phase_ref, amp_ref, tab_ref, *rest,
):
    stage_bufs = rest[: len(stages)]
    in_sem, ex_send, ex_recv, rs_send, rs_recv, ag_send, ag_recv = rest[len(stages) :]
    w = obj_out.shape[-1]
    full = w + 2 * OVL
    loads = [
        pltpu.make_async_copy(src, dst, in_sem.at[i])
        for i, (src, dst) in enumerate(
            (
                (obj_hbm, grad.at[0, pl.ds(0, 4), pl.ds(OVL, w)]),
                (phase_hbm, phase_ref),
                (probe_hbm, probe_ref),
                (tab_hbm, tab_ref),
                (amp_hbm, amp_ref),
            )
        )
    ]
    for load in loads:
        load.start()
    band = 2 * OVL
    row, col = lax.axis_index("row"), lax.axis_index("col")

    def there(dr, dc):
        ok = None
        if dr:
            ok = row > 0 if dr < 0 else row < n_row - 1
        if dc:
            c = col > 0 if dc < 0 else col < n_col - 1
            ok = c if ok is None else jnp.logical_and(ok, c)
        return ok

    def member(group, d):
        if group == "core":
            return row + 1 - 2 * lax.rem(row, 2), col
        if group == "col":
            return row, lax.rem(col + d, n_col)
        n = n_row // 2
        return 2 * lax.rem(lax.div(row, 2) + d, n) + lax.rem(row, 2), col

    def rank(group):
        if group == "core":
            return lax.rem(row, 2)
        return col if group == "col" else lax.div(row, 2)

    barrier = pltpu.get_barrier_semaphore()
    expected = 0
    for dr, dc in SIDES:
        ok = there(dr, dc)
        expected = expected + ok.astype(jnp.int32)

        @pl.when(ok)
        def _():
            pl.semaphore_signal(
                barrier, inc=1, device_id=(row + dr, col + dc), device_id_type=MESH
            )

    for group, n, _, _ in stages:
        for d in range(1, n):
            pl.semaphore_signal(barrier, inc=1, device_id=member(group, d), device_id_type=MESH)
        expected = expected + (n - 1)

    lane = lax.broadcasted_iota(jnp.int32, (full, w), 1)
    line = lax.broadcasted_iota(jnp.int32, (full, w), 0)
    low, high = lane < OVL, lane >= w - OVL
    left_part = high | ((lane >= OVL) & (lane < 2 * OVL))
    top, bottom = row == 0, row == n_row - 1
    row_ok = (jnp.logical_not(top) | (line >= OVL)) & (jnp.logical_not(bottom) | (line < w + OVL))
    at_left, at_right = col == 0, col == n_col - 1
    col_ok = (left_part & jnp.logical_not(at_left)) | (
        jnp.logical_not(left_part) & jnp.logical_not(at_right)
    )
    side_ok = row_ok & col_ok

    def swap(x):
        return pltpu.roll(x, w // 2, x.ndim - 1)

    def rows_of(e, dr):
        if e == 0:
            return {-1: (OVL, OVL), 0: (OVL, w), 1: (w, OVL)}[dr]
        if e == batches:
            return {-1: (0, OVL), 0: (OVL, w), 1: (OVL + w, OVL)}[dr]
        return {-1: (0, band), 0: (0, full), 1: (w, band)}[dr]

    def parts_of(e, k, p):
        dr, dc = SIDES[k]
        first, count = rows_of(e, dr)
        rows, to = pl.ds(first, count), pl.ds(0, count)
        if dc == 0:
            out = [(grad.at[e, pl.ds(2 * p, 2), rows], from_row.at[e, k, pl.ds(2 * p, 2), to], p)]
            if 0 < e < batches:
                out.append((grad.at[e, 4 + p, rows], from_row.at[e, k, 4 + p, to], 2 + p))
            return out
        side = 0 if dc < 0 else 1
        if dr == 0:
            return [(strip.at[e, side, p, rows], from_col.at[e, k - 2, p, to], p)]
        return [(strip.at[e, side, p, rows], from_corner.at[e, k - 4, p, to], p)]

    def copies_of(e, k, p):
        dr, dc = SIDES[k]
        return [
            pltpu.make_async_remote_copy(
                src_ref=src, dst_ref=dst,
                send_sem=ex_send.at[e, k, i], recv_sem=ex_recv.at[e, k, i],
                device_id=(row + dr, col + dc), device_id_type=MESH,
            )
            for src, dst, i in parts_of(e, k, p)
        ]

    def send(e, p):
        side, a, b = grad[e, 4 + p], grad[e, 2 * p], swap(grad[e, 2 * p + 1])
        strip[e, 0, p] = jnp.where(left_part, side, jnp.where(low, a, b))
        strip[e, 1, p] = jnp.where(left_part, jnp.where(high, a, b), side)
        for k in range(8):
            dr, dc = SIDES[k]

            @pl.when(there(dr, dc))
            def _():
                for c in copies_of(e, k, p):
                    c.start()

    def receive(e, scale, p):
        for f in (2 * p, 2 * p + 1, 4 + p):
            ext[f] = ext[f] + scale * grad[e, f] if e else grad[e, f]
        for k in range(8):
            dr, dc = SIDES[k]

            @pl.when(there(-dr, -dc))
            def _():
                for c in copies_of(e, k, p):
                    c.wait_recv()
                first, count = rows_of(e, dr)
                rows = pl.ds(first - dr * w, count)
                if dc == 0:
                    for f in (2 * p, 2 * p + 1) + ((4 + p,) if 0 < e < batches else ()):
                        ext[f, rows] = ext[f, rows] + scale * from_row[e, k, f, :count]
                    return
                lp, lo, hi = left_part[:count], low[:count], high[:count]
                if dr == 0:
                    x = from_col[e, k - 2, p, :count]
                else:
                    x = from_corner[e, k - 4, p, :count]
                x = scale * x
                y = swap(x)
                edge, mine = (lo, lp) if dc > 0 else (hi, jnp.logical_not(lp))
                ext[4 + p, rows] = ext[4 + p, rows] + jnp.where(mine, x, 0.0)
                ext[2 * p, rows] = ext[2 * p, rows] + jnp.where(edge, x, 0.0)
                ext[2 * p + 1, rows] = ext[2 * p + 1, rows] + jnp.where(edge, y, 0.0)

    def sent(e):
        for k in range(8):
            dr, dc = SIDES[k]

            @pl.when(there(dr, dc))
            def _():
                for p in range(2):
                    for c in copies_of(e, k, p):
                        c.wait_send()

    def base_of(s):
        rows = acc.shape[1]
        base = 0
        for group, n, scatter, after in stages[:s]:
            if scatter:
                base = base + rank(group) * after
        return base

    def rs_copies(q, s):
        group, n, scatter, after = stages[s]
        base, mine = base_of(s), rank(group)
        for d in range(1, n):
            to = lax.rem(mine + d, n)
            start = pl.multiple_of(base + (to * after if scatter else 0), 8)
            slot = d - 1 if scatter else mine
            yield pltpu.make_async_remote_copy(
                src_ref=acc.at[q, pl.ds(start, after)], dst_ref=stage_bufs[s].at[q, slot],
                send_sem=rs_send.at[q, s, d], recv_sem=rs_recv.at[q, s, d],
                device_id=member(group, d), device_id_type=MESH,
            )

    def rs_start(q, s):
        for c in rs_copies(q, s):
            c.start()

    def rs_end(q, s):
        group, n, scatter, after = stages[s]
        start = pl.multiple_of(base_of(s + 1), 8)
        place = pl.ds(start, after)
        buf = stage_bufs[s]
        if not scatter:
            buf[q, rank(group)] = acc[q, place]
        for c in rs_copies(q, s):
            c.wait()
        total = acc[q, place] if scatter else buf[q, 0]
        for j in range(0 if scatter else 1, n - 1 if scatter else n):
            total = total + buf[q, j]
        if s == len(stages) - 1:
            gat[q, place] = total
        else:
            acc[q, place] = total

    def ag_copies(q, s):
        group, n, scatter, after = stages[s]
        place = pl.ds(pl.multiple_of(base_of(s + 1), 8), after)
        for d in range(1, n if scatter else 1):
            yield pltpu.make_async_remote_copy(
                src_ref=gat.at[q, place], dst_ref=gat.at[q, place],
                send_sem=ag_send.at[q, s, d], recv_sem=ag_recv.at[q, s, d],
                device_id=member(group, d), device_id_type=MESH,
            )

    def ag_start(q, s):
        for c in ag_copies(q, s):
            c.start()

    def ag_end(q, s):
        for c in ag_copies(q, s):
            c.wait()

    def sum_steps():
        steps = []
        last = len(stages) - 1
        for s in range(last + 1):
            steps.append((lambda i, s=s: rs_start(i, s), lambda i, s=s: rs_end(i, s)))
        for s in range(last, -1, -1):
            steps.append((lambda i, s=s: ag_start(i, s), lambda i, s=s: ag_end(i, s)))
        return steps

    running = []

    def advance():
        for part, steps in list(running):
            steps.pop(0)[1](part)
            if steps:
                steps[0][0](part)
            else:
                running.remove((part, steps))

    def begin(part):
        steps = sum_steps()
        steps[0][0](part)
        running.append((part, steps))

    for f in range(4):
        grad[0, f, :OVL] = jnp.zeros((OVL, w), F32)
        grad[0, f, OVL + w :] = jnp.zeros((OVL, w), F32)
    for f in range(4, 6):
        grad[0, f] = jnp.zeros((full, w), F32)
    loads[0].wait()
    pl.semaphore_wait(barrier, expected)
    send(0, 0)
    send(0, 1)
    for load in loads[1:]:
        load.wait()
    kern_ref[0] = jnp.cos(phase_ref[...])
    kern_ref[1] = jnp.sin(phase_ref[...])
    ziel[...] = jnp.zeros_like(ziel)
    receive(0, 1.0, 0)
    receive(0, 1.0, 1)

    half = modes // 2 if modes % 2 == 0 else modes
    parts = modes // half

    def sum_at(q, m, k):
        return q * parts + m // half, (m % half * 2 + k) * w

    rate = PROBE_RATE / math.sqrt(n_row * n_col)
    kern = (kern_ref[0], kern_ref[1])
    conj_kern = (kern[0], -kern[1])
    tables = ((tab_ref[0], tab_ref[1]), (tab_ref[2], tab_ref[3]))
    lane_w = lax.broadcasted_iota(jnp.int32, (w, w), 1)

    for b in range(batches):
        if b == 0 or b == 1:
            source = probe_ref
        else:
            while running:
                advance()
            previous = probe_ref if b == 2 else pnow
            for m in range(modes):
                for k in range(2):
                    i, at = sum_at(b - 2, m, k)
                    pnow[m, k] = previous[m, k] - rate * gat[i, at : at + w]
            source = pnow
        y0, x0 = off_ref[b, 0], off_ref[b, 1]
        start = x0 - OVL
        back = lax.rem(w - start, w)
        back_half = lax.rem(w + w // 2 - start, w)
        inside = (lane_w + start >= 0) & (lane_w + start < w)

        def window(f):
            main = ext[f, pl.ds(y0, w), :]
            side = ext[4 + f // 2, pl.ds(y0, w), :]
            return jnp.where(
                inside,
                pltpu.roll(main, back, 1),
                pltpu.roll(side, back_half if f % 2 else back, 1),
            )

        o1, o2 = (window(0), window(1)), (window(2), window(3))
        probe = [(source[m, 0], source[m, 1]) for m in range(modes)]
        spectrum = dft([cmul(p, o1) for p in probe], tables, False)
        phi = dft([cmul(v, kern) for v in spectrum], tables, True)
        for m in range(modes):
            phi_ref[m, 0], phi_ref[m, 1] = phi[m]
        advance()
        far = dft([cmul(v, o2) for v in phi], tables, False)
        intensity = far[0][0] * far[0][0] + far[0][1] * far[0][1]
        for v in far[1:]:
            intensity = intensity + (v[0] * v[0] + v[1] * v[1])
        factor = 1.0 - amp_ref[b] / jnp.sqrt(intensity + FLOOR)
        chi2 = dft([(v[0] * factor, v[1] * factor) for v in far], tables, True)
        advance()
        g2 = csum([conj_mul((phi_ref[m, 0], phi_ref[m, 1]), chi2[m]) for m in range(modes)])
        ahead = lax.rem(w + start, w)
        outside = (lane - start < 0) | (lane - start >= w)

        def place(p, pair):
            others = []
            for f in (2 * p, 2 * p + 1):
                ziel[f, 2 * OVL : 2 * OVL + w] = pair[f % 2]
                moved = pltpu.roll(ziel[f, pl.ds(2 * OVL - y0, full), :], ahead, 1)
                grad[b + 1, f] = jnp.where(row_ok & jnp.logical_not(outside), moved, 0.0)
                others.append(jnp.where(outside, moved, 0.0))
            grad[b + 1, 4 + p] = jnp.where(side_ok, others[0] + swap(others[1]), 0.0)
            send(b + 1, p)

        place(1, g2)
        q = min(b, max(batches - 2, 0))
        final = b == batches - 1
        starts_sum = b != batches - 2 or batches == 1
        g1 = None

        def keep(group, chi1):
            for m, v in zip(group, chi1):
                g = conj_mul(o1, v)
                for k in range(2):
                    i, at = sum_at(q, m, k)
                    place_at = pl.ds(at, w)
                    acc[i, place_at] = g[k] if b == q else acc[i, place_at] + g[k]

        kept = []
        for part in range(parts):
            group = range(part * half, part * half + half)
            spectrum = dft([conj_mul(o2, chi2[m]) for m in group], tables, False)
            chi1 = dft([cmul(v, conj_kern) for v in spectrum], tables, True)
            if final:
                keep(group, chi1)
                if part:
                    advance()
                begin(q * parts + part)
            else:
                kept.append((group, chi1))
            term = csum(
                [conj_mul((source[m, 0], source[m, 1]), v) for m, v in zip(group, chi1)]
            )
            g1 = term if g1 is None else csum([g1, term])
        if not final:
            advance()
        place(0, g1)
        advance()
        for group, chi1 in kept:
            keep(group, chi1)
        if starts_sum and not final:
            while running:
                advance()
            for part in range(parts):
                begin(q * parts + part)
        receive(b + 1, -OBJECT_RATE, 1)
        if final:
            advance()
        receive(b + 1, -OBJECT_RATE, 0)
        advance()
        if final:
            for f in range(4):
                obj_out[f] = ext[f, OVL : OVL + w]

    while running:
        advance()
    q = max(batches - 2, 0)
    last = pnow if batches > 2 else probe_ref
    for m in range(modes):
        for k in range(2):
            i, at = sum_at(q, m, k)
            probe_out[m, k] = last[m, k] - rate * gat[i, at : at + w]
    for e in range(batches + 1):
        sent(e)


def per_device(n_row, n_col, object_field, probe, kernel_phase, amplitudes, offsets):
    batches = amplitudes.shape[0]
    modes, _, w, _ = probe.shape
    full = w + 2 * OVL
    parts = 2 if modes % 2 == 0 else 1
    rows = modes * 2 * w // parts
    stages = stages_of(rows, n_row, n_col)
    sums = max(batches - 1, 1) * parts
    most = max(n for _, n, _, _ in stages)
    vmem, smem = pltpu.VMEM, pltpu.SMEM
    dma = pltpu.SemaphoreType.DMA
    scratch = [
        vmem((6, full, w), F32),
        vmem((4, full + 2 * OVL, w), F32),
        vmem((batches + 1, 6, full, w), F32),
        vmem((batches + 1, 2, 2, full, w), F32),
        vmem((batches + 1, 2, 6, 2 * OVL, w), F32),
        vmem((batches + 1, 2, 2, full, w), F32),
        vmem((batches + 1, 4, 2, 2 * OVL, w), F32),
        vmem((modes, 2, w, w), F32),
        vmem((2, w, w), F32),
        vmem((modes, 2, w, w), F32),
        vmem((sums, rows, w), F32),
        vmem((sums, rows, w), F32),
        vmem(probe.shape, F32),
        vmem((w, w), F32),
        vmem((batches, w, w), F32),
        vmem((4, 2 * w, 2 * w), BF16),
    ]
    for _, n, scatter, after in stages:
        scratch.append(vmem((sums, n - 1 if scatter else n, after, w), F32))
    scratch += [dma((5,))] + [dma((batches + 1, 8, 4))] * 2 + [dma((sums, len(stages), most))] * 4
    whole = pl.BlockSpec(memory_space=vmem)
    obj, new_probe = pl.pallas_call(
        functools.partial(kernel, n_row, n_col, batches, modes, stages),
        out_shape=(
            jax.ShapeDtypeStruct((4, w, w), F32),
            jax.ShapeDtypeStruct(probe.shape, F32),
        ),
        in_specs=[pl.BlockSpec(memory_space=smem)] + [pl.BlockSpec(memory_space=pltpu.HBM)] * 5,
        out_specs=(whole, whole),
        scratch_shapes=scratch,
        compiler_params=pltpu.CompilerParams(
            collective_id=0, has_side_effects=True, vmem_limit_bytes=48 * 2**20
        ),
    )(
        offsets.reshape(batches, 2),
        object_field.reshape(4, w, w),
        probe,
        kernel_phase,
        amplitudes.reshape(batches, w, w),
        jnp.asarray(dft_matrices(w)),
    )
    return obj.reshape(object_field.shape), new_probe


def solution(mesh):
    in_specs = (
        P(None, None, "row", "col"),
        P(),
        P(),
        P(None, "row", "col", None, None),
        P(None, "row", "col", None),
    )
    out_specs = (P(None, None, "row", "col"), P())
    return jax.shard_map(
        functools.partial(per_device, mesh.shape["row"], mesh.shape["col"]),
        mesh=mesh, in_specs=in_specs, out_specs=out_specs, check_vma=False,
    )
```

```python
import functools
import math

import jax
import jax.numpy as jnp
import numpy as np
from jax import lax
from jax.experimental import pallas as pl
from jax.experimental.pallas import tpu as pltpu
from jax.sharding import PartitionSpec as P

OVL = 32
OBJECT_RATE = 0.5
PROBE_RATE = 0.5
FLOOR = 0.1
MESH = pl.DeviceIdType.MESH
F32 = jnp.float32
BF16 = jnp.bfloat16

SIDES = ((-1, 0), (1, 0), (0, -1), (0, 1), (-1, -1), (-1, 1), (1, -1), (1, 1))


def split(values):
    high = values.astype(BF16)
    return high, (values - high.astype(F32)).astype(BF16)


def dft_matrices(window):
    counter = np.arange(window)
    phases = (counter[:, None] * counter[None, :] % window) * (-2.0 * np.pi / window)
    c, s = np.cos(phases) / math.sqrt(window), np.sin(phases) / math.sqrt(window)
    left = np.block([[c, -s], [s, c]]).astype(np.float32)
    out = []
    for m in (left, left.T):
        high = m.astype(BF16)
        out += [high, (m - high.astype(np.float32)).astype(BF16)]
    return np.stack(out)


def dot(a, b):
    return jnp.dot(a, b, preferred_element_type=F32)


def product(a, b):
    return dot(a[0], b[0]) + (dot(a[0], b[1]) + dot(a[1], b[0]))


def dft(fields, tables, inverse):
    first, second = (tables[1], tables[0]) if inverse else tables
    w = fields[0][0].shape[0]
    x = jnp.concatenate(
        [jnp.concatenate([f[k] for f in fields], axis=1) for k in range(2)], axis=0
    )
    y = product(first, split(x))
    z = jnp.concatenate(
        [
            jnp.concatenate([y[:w, m * w : m * w + w], y[w:, m * w : m * w + w]], axis=1)
            for m in range(len(fields))
        ],
        axis=0,
    )
    r = product(split(z), second)
    return [(r[m * w : m * w + w, :w], r[m * w : m * w + w, w:]) for m in range(len(fields))]


def cmul(a, b):
    return a[0] * b[0] - a[1] * b[1], a[0] * b[1] + a[1] * b[0]


def conj_mul(a, b):
    return a[0] * b[0] + a[1] * b[1], a[0] * b[1] - a[1] * b[0]


def csum(pairs):
    re, im = pairs[0]
    for p in pairs[1:]:
        re, im = re + p[0], im + p[1]
    return re, im


def stages_of(rows, n_row, n_col):
    out = []
    for group, n in (("core", 2), ("col", n_col), ("rest", n_row // 2)):
        if n < 2:
            continue
        scatter = rows % (8 * n) == 0
        rows = rows // n if scatter else rows
        out.append((group, n, scatter, rows))
    return out


def kernel(
    n_row, n_col, batches, modes, stages,
    off_ref, obj_hbm, probe_hbm, phase_hbm, amp_hbm, tab_hbm,
    obj_out, probe_out,
    ext, ziel, grad, strip, from_row, from_col, from_corner,
    phi_ref, kern_ref, pnow, acc, gat, probe_ref, phase_ref, amp_ref, tab_ref, *rest,
):
    stage_bufs = rest[: len(stages)]
    in_sem, ex_send, ex_recv, rs_send, rs_recv, ag_send, ag_recv = rest[len(stages) :]
    w = obj_out.shape[-1]
    full = w + 2 * OVL
    loads = [
        pltpu.make_async_copy(src, dst, in_sem.at[i])
        for i, (src, dst) in enumerate(
            (
                (obj_hbm, grad.at[0, pl.ds(0, 4), pl.ds(OVL, w)]),
                (phase_hbm, phase_ref),
                (probe_hbm, probe_ref),
                (tab_hbm, tab_ref),
                (amp_hbm, amp_ref),
            )
        )
    ]
    for load in loads:
        load.start()
    band = 2 * OVL
    row, col = lax.axis_index("row"), lax.axis_index("col")

    def there(dr, dc):
        ok = None
        if dr:
            ok = row > 0 if dr < 0 else row < n_row - 1
        if dc:
            c = col > 0 if dc < 0 else col < n_col - 1
            ok = c if ok is None else jnp.logical_and(ok, c)
        return ok

    def member(group, d):
        if group == "core":
            return row + 1 - 2 * lax.rem(row, 2), col
        if group == "col":
            return row, lax.rem(col + d, n_col)
        n = n_row // 2
        return 2 * lax.rem(lax.div(row, 2) + d, n) + lax.rem(row, 2), col

    def rank(group):
        if group == "core":
            return lax.rem(row, 2)
        return col if group == "col" else lax.div(row, 2)

    barrier = pltpu.get_barrier_semaphore()
    expected = 0
    for dr, dc in SIDES:
        ok = there(dr, dc)
        expected = expected + ok.astype(jnp.int32)

        @pl.when(ok)
        def _():
            pl.semaphore_signal(
                barrier, inc=1, device_id=(row + dr, col + dc), device_id_type=MESH
            )

    for group, n, _, _ in stages:
        for d in range(1, n):
            pl.semaphore_signal(barrier, inc=1, device_id=member(group, d), device_id_type=MESH)
        expected = expected + (n - 1)

    lane = lax.broadcasted_iota(jnp.int32, (full, w), 1)
    line = lax.broadcasted_iota(jnp.int32, (full, w), 0)
    low, high = lane < OVL, lane >= w - OVL
    left_part = high | ((lane >= OVL) & (lane < 2 * OVL))
    top, bottom = row == 0, row == n_row - 1
    row_ok = (jnp.logical_not(top) | (line >= OVL)) & (jnp.logical_not(bottom) | (line < w + OVL))
    at_left, at_right = col == 0, col == n_col - 1
    col_ok = (left_part & jnp.logical_not(at_left)) | (
        jnp.logical_not(left_part) & jnp.logical_not(at_right)
    )
    side_ok = row_ok & col_ok

    def swap(x):
        return pltpu.roll(x, w // 2, x.ndim - 1)

    def rows_of(e, dr):
        if e == 0:
            return {-1: (OVL, OVL), 0: (OVL, w), 1: (w, OVL)}[dr]
        if e == batches:
            return {-1: (0, OVL), 0: (OVL, w), 1: (OVL + w, OVL)}[dr]
        return {-1: (0, band), 0: (0, full), 1: (w, band)}[dr]

    def parts_of(e, k, p):
        dr, dc = SIDES[k]
        first, count = rows_of(e, dr)
        rows, to = pl.ds(first, count), pl.ds(0, count)
        if dc == 0:
            out = [(grad.at[e, pl.ds(2 * p, 2), rows], from_row.at[e, k, pl.ds(2 * p, 2), to], p)]
            if 0 < e < batches:
                out.append((grad.at[e, 4 + p, rows], from_row.at[e, k, 4 + p, to], 2 + p))
            return out
        side = 0 if dc < 0 else 1
        if dr == 0:
            return [(strip.at[e, side, p, rows], from_col.at[e, k - 2, p, to], p)]
        return [(strip.at[e, side, p, rows], from_corner.at[e, k - 4, p, to], p)]

    def copies_of(e, k, p):
        dr, dc = SIDES[k]
        return [
            pltpu.make_async_remote_copy(
                src_ref=src, dst_ref=dst,
                send_sem=ex_send.at[e, k, i], recv_sem=ex_recv.at[e, k, i],
                device_id=(row + dr, col + dc), device_id_type=MESH,
            )
            for src, dst, i in parts_of(e, k, p)
        ]

    def send(e, p):
        side, a, b = grad[e, 4 + p], grad[e, 2 * p], swap(grad[e, 2 * p + 1])
        strip[e, 0, p] = jnp.where(left_part, side, jnp.where(low, a, b))
        strip[e, 1, p] = jnp.where(left_part, jnp.where(high, a, b), side)
        for k in range(8):
            dr, dc = SIDES[k]

            @pl.when(there(dr, dc))
            def _():
                for c in copies_of(e, k, p):
                    c.start()

    def receive(e, scale, p):
        for f in (2 * p, 2 * p + 1, 4 + p):
            ext[f] = ext[f] + scale * grad[e, f] if e else grad[e, f]
        for k in range(8):
            dr, dc = SIDES[k]

            @pl.when(there(-dr, -dc))
            def _():
                for c in copies_of(e, k, p):
                    c.wait_recv()
                first, count = rows_of(e, dr)
                rows = pl.ds(first - dr * w, count)
                if dc == 0:
                    for f in (2 * p, 2 * p + 1) + ((4 + p,) if 0 < e < batches else ()):
                        ext[f, rows] = ext[f, rows] + scale * from_row[e, k, f, :count]
                    return
                lp, lo, hi = left_part[:count], low[:count], high[:count]
                if dr == 0:
                    x = from_col[e, k - 2, p, :count]
                else:
                    x = from_corner[e, k - 4, p, :count]
                x = scale * x
                y = swap(x)
                edge, mine = (lo, lp) if dc > 0 else (hi, jnp.logical_not(lp))
                ext[4 + p, rows] = ext[4 + p, rows] + jnp.where(mine, x, 0.0)
                ext[2 * p, rows] = ext[2 * p, rows] + jnp.where(edge, x, 0.0)
                ext[2 * p + 1, rows] = ext[2 * p + 1, rows] + jnp.where(edge, y, 0.0)

    def sent(e):
        for k in range(8):
            dr, dc = SIDES[k]

            @pl.when(there(dr, dc))
            def _():
                for p in range(2):
                    for c in copies_of(e, k, p):
                        c.wait_send()

    def base_of(s):
        rows = acc.shape[1]
        base = 0
        for group, n, scatter, after in stages[:s]:
            if scatter:
                base = base + rank(group) * after
        return base

    def rs_copies(q, s):
        group, n, scatter, after = stages[s]
        base, mine = base_of(s), rank(group)
        for d in range(1, n):
            to = lax.rem(mine + d, n)
            start = pl.multiple_of(base + (to * after if scatter else 0), 8)
            slot = d - 1 if scatter else mine
            yield pltpu.make_async_remote_copy(
                src_ref=acc.at[q, pl.ds(start, after)], dst_ref=stage_bufs[s].at[q, slot],
                send_sem=rs_send.at[q, s, d], recv_sem=rs_recv.at[q, s, d],
                device_id=member(group, d), device_id_type=MESH,
            )

    def rs_start(q, s):
        for c in rs_copies(q, s):
            c.start()

    def rs_end(q, s):
        group, n, scatter, after = stages[s]
        start = pl.multiple_of(base_of(s + 1), 8)
        place = pl.ds(start, after)
        buf = stage_bufs[s]
        if not scatter:
            buf[q, rank(group)] = acc[q, place]
        for c in rs_copies(q, s):
            c.wait()
        total = acc[q, place] if scatter else buf[q, 0]
        for j in range(0 if scatter else 1, n - 1 if scatter else n):
            total = total + buf[q, j]
        if s == len(stages) - 1:
            gat[q, place] = total
        else:
            acc[q, place] = total

    def ag_copies(q, s):
        group, n, scatter, after = stages[s]
        place = pl.ds(pl.multiple_of(base_of(s + 1), 8), after)
        for d in range(1, n if scatter else 1):
            yield pltpu.make_async_remote_copy(
                src_ref=gat.at[q, place], dst_ref=gat.at[q, place],
                send_sem=ag_send.at[q, s, d], recv_sem=ag_recv.at[q, s, d],
                device_id=member(group, d), device_id_type=MESH,
            )

    def ag_start(q, s):
        for c in ag_copies(q, s):
            c.start()

    def ag_end(q, s):
        for c in ag_copies(q, s):
            c.wait()

    def sum_steps():
        steps = []
        last = len(stages) - 1
        for s in range(last + 1):
            steps.append((lambda i, s=s: rs_start(i, s), lambda i, s=s: rs_end(i, s)))
        for s in range(last, -1, -1):
            steps.append((lambda i, s=s: ag_start(i, s), lambda i, s=s: ag_end(i, s)))
        return steps

    running = []

    def advance():
        for part, steps in list(running):
            steps.pop(0)[1](part)
            if steps:
                steps[0][0](part)
            else:
                running.remove((part, steps))

    def begin(part):
        steps = sum_steps()
        steps[0][0](part)
        running.append((part, steps))

    for f in range(4):
        grad[0, f, :OVL] = jnp.zeros((OVL, w), F32)
        grad[0, f, OVL + w :] = jnp.zeros((OVL, w), F32)
    for f in range(4, 6):
        grad[0, f] = jnp.zeros((full, w), F32)
    loads[0].wait()
    pl.semaphore_wait(barrier, expected)
    send(0, 0)
    send(0, 1)
    for load in loads[1:]:
        load.wait()
    kern_ref[0] = jnp.cos(phase_ref[...])
    kern_ref[1] = jnp.sin(phase_ref[...])
    ziel[...] = jnp.zeros_like(ziel)
    receive(0, 1.0, 0)
    receive(0, 1.0, 1)

    half = modes // 2 if modes % 2 == 0 else modes
    parts = modes // half

    def sum_at(q, m, k):
        return q * parts + m // half, (m % half * 2 + k) * w

    rate = PROBE_RATE / math.sqrt(n_row * n_col)
    kern = (kern_ref[0], kern_ref[1])
    conj_kern = (kern[0], -kern[1])
    tables = ((tab_ref[0], tab_ref[1]), (tab_ref[2], tab_ref[3]))
    lane_w = lax.broadcasted_iota(jnp.int32, (w, w), 1)

    for b in range(batches):
        if b == 0 or b == 1:
            source = probe_ref
        else:
            while running:
                advance()
            previous = probe_ref if b == 2 else pnow
            for m in range(modes):
                for k in range(2):
                    i, at = sum_at(b - 2, m, k)
                    pnow[m, k] = previous[m, k] - rate * gat[i, at : at + w]
            source = pnow
        y0, x0 = off_ref[b, 0], off_ref[b, 1]
        start = x0 - OVL
        back = lax.rem(w - start, w)
        back_half = lax.rem(w + w // 2 - start, w)
        inside = (lane_w + start >= 0) & (lane_w + start < w)

        def window(f):
            main = ext[f, pl.ds(y0, w), :]
            side = ext[4 + f // 2, pl.ds(y0, w), :]
            return jnp.where(
                inside,
                pltpu.roll(main, back, 1),
                pltpu.roll(side, back_half if f % 2 else back, 1),
            )

        o1, o2 = (window(0), window(1)), (window(2), window(3))
        probe = [(source[m, 0], source[m, 1]) for m in range(modes)]
        spectrum = dft([cmul(p, o1) for p in probe], tables, False)
        phi = dft([cmul(v, kern) for v in spectrum], tables, True)
        for m in range(modes):
            phi_ref[m, 0], phi_ref[m, 1] = phi[m]
        advance()
        far = dft([cmul(v, o2) for v in phi], tables, False)
        intensity = far[0][0] * far[0][0] + far[0][1] * far[0][1]
        for v in far[1:]:
            intensity = intensity + (v[0] * v[0] + v[1] * v[1])
        factor = 1.0 - amp_ref[b] / jnp.sqrt(intensity + FLOOR)
        chi2 = dft([(v[0] * factor, v[1] * factor) for v in far], tables, True)
        advance()
        g2 = csum([conj_mul((phi_ref[m, 0], phi_ref[m, 1]), chi2[m]) for m in range(modes)])
        ahead = lax.rem(w + start, w)
        outside = (lane - start < 0) | (lane - start >= w)

        def place(p, pair):
            others = []
            for f in (2 * p, 2 * p + 1):
                ziel[f, 2 * OVL : 2 * OVL + w] = pair[f % 2]
                moved = pltpu.roll(ziel[f, pl.ds(2 * OVL - y0, full), :], ahead, 1)
                grad[b + 1, f] = jnp.where(row_ok & jnp.logical_not(outside), moved, 0.0)
                others.append(jnp.where(outside, moved, 0.0))
            grad[b + 1, 4 + p] = jnp.where(side_ok, others[0] + swap(others[1]), 0.0)
            send(b + 1, p)

        place(1, g2)
        q = min(b, max(batches - 2, 0))
        final = b == batches - 1
        starts_sum = b != batches - 2 or batches == 1
        g1 = None

        def keep(group, chi1):
            for m, v in zip(group, chi1):
                g = conj_mul(o1, v)
                for k in range(2):
                    i, at = sum_at(q, m, k)
                    place_at = pl.ds(at, w)
                    acc[i, place_at] = g[k] if b == q else acc[i, place_at] + g[k]

        kept = []
        for part in range(parts):
            group = range(part * half, part * half + half)
            spectrum = dft([conj_mul(o2, chi2[m]) for m in group], tables, False)
            chi1 = dft([cmul(v, conj_kern) for v in spectrum], tables, True)
            if final:
                keep(group, chi1)
                if part:
                    advance()
                begin(q * parts + part)
            else:
                kept.append((group, chi1))
            term = csum(
                [conj_mul((source[m, 0], source[m, 1]), v) for m, v in zip(group, chi1)]
            )
            g1 = term if g1 is None else csum([g1, term])
        if not final:
            advance()
        place(0, g1)
        advance()
        for group, chi1 in kept:
            keep(group, chi1)
        if starts_sum and not final:
            while running:
                advance()
            for part in range(parts):
                begin(q * parts + part)
        receive(b + 1, -OBJECT_RATE, 1)
        if final:
            advance()
        receive(b + 1, -OBJECT_RATE, 0)
        advance()
        if final:
            for f in range(4):
                obj_out[f] = ext[f, OVL : OVL + w]

    while running:
        advance()
    q = max(batches - 2, 0)
    last = pnow if batches > 2 else probe_ref
    for m in range(modes):
        for k in range(2):
            i, at = sum_at(q, m, k)
            probe_out[m, k] = last[m, k] - rate * gat[i, at : at + w]
    for e in range(batches + 1):
        sent(e)


def per_device(n_row, n_col, object_field, probe, kernel_phase, amplitudes, offsets):
    batches = amplitudes.shape[0]
    modes, _, w, _ = probe.shape
    full = w + 2 * OVL
    parts = 2 if modes % 2 == 0 else 1
    rows = modes * 2 * w // parts
    stages = stages_of(rows, n_row, n_col)
    sums = max(batches - 1, 1) * parts
    most = max(n for _, n, _, _ in stages)
    vmem, smem = pltpu.VMEM, pltpu.SMEM
    dma = pltpu.SemaphoreType.DMA
    scratch = [
        vmem((6, full, w), F32),
        vmem((4, full + 2 * OVL, w), F32),
        vmem((batches + 1, 6, full, w), F32),
        vmem((batches + 1, 2, 2, full, w), F32),
        vmem((batches + 1, 2, 6, 2 * OVL, w), F32),
        vmem((batches + 1, 2, 2, full, w), F32),
        vmem((batches + 1, 4, 2, 2 * OVL, w), F32),
        vmem((modes, 2, w, w), F32),
        vmem((2, w, w), F32),
        vmem((modes, 2, w, w), F32),
        vmem((sums, rows, w), F32),
        vmem((sums, rows, w), F32),
        vmem(probe.shape, F32),
        vmem((w, w), F32),
        vmem((batches, w, w), F32),
        vmem((4, 2 * w, 2 * w), BF16),
    ]
    for _, n, scatter, after in stages:
        scratch.append(vmem((sums, n - 1 if scatter else n, after, w), F32))
    scratch += [dma((5,))] + [dma((batches + 1, 8, 4))] * 2 + [dma((sums, len(stages), most))] * 4
    whole = pl.BlockSpec(memory_space=vmem)
    obj, new_probe = pl.pallas_call(
        functools.partial(kernel, n_row, n_col, batches, modes, stages),
        out_shape=(
            jax.ShapeDtypeStruct((4, w, w), F32),
            jax.ShapeDtypeStruct(probe.shape, F32),
        ),
        in_specs=[pl.BlockSpec(memory_space=smem)] + [pl.BlockSpec(memory_space=pltpu.HBM)] * 5,
        out_specs=(whole, whole),
        scratch_shapes=scratch,
        compiler_params=pltpu.CompilerParams(
            collective_id=0, has_side_effects=True, vmem_limit_bytes=64 * 2**20 - 64 * 2**10
        ),
    )(
        offsets.reshape(batches, 2),
        object_field.reshape(4, w, w),
        probe,
        kernel_phase,
        amplitudes.reshape(batches, w, w),
        jnp.asarray(dft_matrices(w)),
    )
    return obj.reshape(object_field.shape), new_probe


def solution(mesh):
    in_specs = (
        P(None, None, "row", "col"),
        P(),
        P(),
        P(None, "row", "col", None, None),
        P(None, "row", "col", None),
    )
    out_specs = (P(None, None, "row", "col"), P())
    return jax.shard_map(
        functools.partial(per_device, mesh.shape["row"], mesh.shape["col"]),
        mesh=mesh, in_specs=in_specs, out_specs=out_specs, check_vma=False,
    )
```

```python
import functools
import math

import jax
import jax.numpy as jnp
import numpy as np
from jax import lax
from jax.experimental import pallas as pl
from jax.experimental.pallas import tpu as pltpu
from jax.sharding import PartitionSpec as P

OVL = 32
OBJECT_RATE = 0.5
PROBE_RATE = 0.5
FLOOR = 0.1
MESH = pl.DeviceIdType.MESH
F32 = jnp.float32
BF16 = jnp.bfloat16

SIDES = ((-1, 0), (1, 0), (0, -1), (0, 1), (-1, -1), (-1, 1), (1, -1), (1, 1))


def split(values):
    high = values.astype(BF16)
    return high, (values - high.astype(F32)).astype(BF16)


def dft_matrices(window):
    counter = np.arange(window)
    phases = (counter[:, None] * counter[None, :] % window) * (-2.0 * np.pi / window)
    c, s = np.cos(phases) / math.sqrt(window), np.sin(phases) / math.sqrt(window)
    left = np.block([[c, -s], [s, c]]).astype(np.float32)
    out = []
    for m in (left, left.T):
        high = m.astype(BF16)
        out += [high, (m - high.astype(np.float32)).astype(BF16)]
    return np.stack(out)


def dot(a, b):
    return jnp.dot(a, b, preferred_element_type=F32)


def product(a, b):
    return dot(a[0], b[0]) + (dot(a[0], b[1]) + dot(a[1], b[0]))


def dft(fields, tables, inverse):
    first, second = (tables[1], tables[0]) if inverse else tables
    w = fields[0][0].shape[0]
    x = jnp.concatenate(
        [jnp.concatenate([f[k] for f in fields], axis=1) for k in range(2)], axis=0
    )
    y = product(first, split(x))
    z = jnp.concatenate(
        [
            jnp.concatenate([y[:w, m * w : m * w + w], y[w:, m * w : m * w + w]], axis=1)
            for m in range(len(fields))
        ],
        axis=0,
    )
    r = product(split(z), second)
    return [(r[m * w : m * w + w, :w], r[m * w : m * w + w, w:]) for m in range(len(fields))]


def cmul(a, b):
    return a[0] * b[0] - a[1] * b[1], a[0] * b[1] + a[1] * b[0]


def conj_mul(a, b):
    return a[0] * b[0] + a[1] * b[1], a[0] * b[1] - a[1] * b[0]


def csum(pairs):
    re, im = pairs[0]
    for p in pairs[1:]:
        re, im = re + p[0], im + p[1]
    return re, im


def stages_of(rows, n_row, n_col):
    out = []
    for group, n in (("core", 2), ("col", n_col), ("rest", n_row // 2)):
        if n < 2:
            continue
        scatter = rows % (8 * n) == 0
        rows = rows // n if scatter else rows
        out.append((group, n, scatter, rows))
    return out


def kernel(
    n_row, n_col, batches, modes, stages,
    off_ref, obj_hbm, probe_hbm, phase_hbm, amp_hbm, tab_hbm,
    obj_out, probe_out,
    ext, ziel, grad, strip, from_row, from_col, from_corner,
    phi_ref, kern_ref, pnow, acc, gat, probe_ref, phase_ref, amp_ref, tab_ref, *rest,
):
    stage_bufs = rest[: len(stages)]
    in_sem, ex_send, ex_recv, rs_send, rs_recv, ag_send, ag_recv = rest[len(stages) :]
    w = obj_out.shape[-1]
    full = w + 2 * OVL
    loads = [
        pltpu.make_async_copy(src, dst, in_sem.at[i])
        for i, (src, dst) in enumerate(
            (
                (obj_hbm, grad.at[0, pl.ds(0, 4), pl.ds(OVL, w)]),
                (phase_hbm, phase_ref),
                (probe_hbm, probe_ref),
                (tab_hbm, tab_ref),
                (amp_hbm, amp_ref),
            )
        )
    ]
    for load in loads:
        load.start()
    band = 2 * OVL
    row, col = lax.axis_index("row"), lax.axis_index("col")

    def there(dr, dc):
        ok = None
        if dr:
            ok = row > 0 if dr < 0 else row < n_row - 1
        if dc:
            c = col > 0 if dc < 0 else col < n_col - 1
            ok = c if ok is None else jnp.logical_and(ok, c)
        return ok

    def member(group, d):
        if group == "core":
            return row + 1 - 2 * lax.rem(row, 2), col
        if group == "col":
            return row, lax.rem(col + d, n_col)
        n = n_row // 2
        return 2 * lax.rem(lax.div(row, 2) + d, n) + lax.rem(row, 2), col

    def rank(group):
        if group == "core":
            return lax.rem(row, 2)
        return col if group == "col" else lax.div(row, 2)

    barrier = pltpu.get_barrier_semaphore()
    expected = 0
    for dr, dc in SIDES:
        ok = there(dr, dc)
        expected = expected + ok.astype(jnp.int32)

        @pl.when(ok)
        def _():
            pl.semaphore_signal(
                barrier, inc=1, device_id=(row + dr, col + dc), device_id_type=MESH
            )

    for group, n, _, _ in stages:
        for d in range(1, n):
            pl.semaphore_signal(barrier, inc=1, device_id=member(group, d), device_id_type=MESH)
        expected = expected + (n - 1)

    lane = lax.broadcasted_iota(jnp.int32, (full, w), 1)
    line = lax.broadcasted_iota(jnp.int32, (full, w), 0)
    low, high = lane < OVL, lane >= w - OVL
    left_part = high | ((lane >= OVL) & (lane < 2 * OVL))
    top, bottom = row == 0, row == n_row - 1
    row_ok = (jnp.logical_not(top) | (line >= OVL)) & (jnp.logical_not(bottom) | (line < w + OVL))
    at_left, at_right = col == 0, col == n_col - 1
    col_ok = (left_part & jnp.logical_not(at_left)) | (
        jnp.logical_not(left_part) & jnp.logical_not(at_right)
    )
    side_ok = row_ok & col_ok

    def swap(x):
        return pltpu.roll(x, w // 2, x.ndim - 1)

    def rows_of(e, dr):
        if e == 0:
            return {-1: (OVL, OVL), 0: (OVL, w), 1: (w, OVL)}[dr]
        if e == batches:
            return {-1: (0, OVL), 0: (OVL, w), 1: (OVL + w, OVL)}[dr]
        return {-1: (0, band), 0: (0, full), 1: (w, band)}[dr]

    def parts_of(e, k, p):
        dr, dc = SIDES[k]
        first, count = rows_of(e, dr)
        rows, to = pl.ds(first, count), pl.ds(0, count)
        if dc == 0:
            out = [(grad.at[e, pl.ds(2 * p, 2), rows], from_row.at[e, k, pl.ds(2 * p, 2), to], p)]
            if 0 < e < batches:
                out.append((grad.at[e, 4 + p, rows], from_row.at[e, k, 4 + p, to], 2 + p))
            return out
        side = 0 if dc < 0 else 1
        if dr == 0:
            return [(strip.at[e, side, p, rows], from_col.at[e, k - 2, p, to], p)]
        return [(strip.at[e, side, p, rows], from_corner.at[e, k - 4, p, to], p)]

    def copies_of(e, k, p):
        dr, dc = SIDES[k]
        return [
            pltpu.make_async_remote_copy(
                src_ref=src, dst_ref=dst,
                send_sem=ex_send.at[e, k, i], recv_sem=ex_recv.at[e, k, i],
                device_id=(row + dr, col + dc), device_id_type=MESH,
            )
            for src, dst, i in parts_of(e, k, p)
        ]

    def send(e, p):
        side, a, b = grad[e, 4 + p], grad[e, 2 * p], swap(grad[e, 2 * p + 1])
        strip[e, 0, p] = jnp.where(left_part, side, jnp.where(low, a, b))
        strip[e, 1, p] = jnp.where(left_part, jnp.where(high, a, b), side)
        for k in range(8):
            dr, dc = SIDES[k]

            @pl.when(there(dr, dc))
            def _():
                for c in copies_of(e, k, p):
                    c.start()

    def receive(e, scale, p):
        for f in (2 * p, 2 * p + 1, 4 + p):
            ext[f] = ext[f] + scale * grad[e, f] if e else grad[e, f]
        for k in range(8):
            dr, dc = SIDES[k]

            @pl.when(there(-dr, -dc))
            def _():
                for c in copies_of(e, k, p):
                    c.wait_recv()
                first, count = rows_of(e, dr)
                rows = pl.ds(first - dr * w, count)
                if dc == 0:
                    for f in (2 * p, 2 * p + 1) + ((4 + p,) if 0 < e < batches else ()):
                        ext[f, rows] = ext[f, rows] + scale * from_row[e, k, f, :count]
                    return
                lp, lo, hi = left_part[:count], low[:count], high[:count]
                if dr == 0:
                    x = from_col[e, k - 2, p, :count]
                else:
                    x = from_corner[e, k - 4, p, :count]
                x = scale * x
                y = swap(x)
                edge, mine = (lo, lp) if dc > 0 else (hi, jnp.logical_not(lp))
                ext[4 + p, rows] = ext[4 + p, rows] + jnp.where(mine, x, 0.0)
                ext[2 * p, rows] = ext[2 * p, rows] + jnp.where(edge, x, 0.0)
                ext[2 * p + 1, rows] = ext[2 * p + 1, rows] + jnp.where(edge, y, 0.0)

    def sent(e):
        for k in range(8):
            dr, dc = SIDES[k]

            @pl.when(there(dr, dc))
            def _():
                for p in range(2):
                    for c in copies_of(e, k, p):
                        c.wait_send()

    def base_of(s):
        rows = acc.shape[1]
        base = 0
        for group, n, scatter, after in stages[:s]:
            if scatter:
                base = base + rank(group) * after
        return base

    def rs_copies(q, s):
        group, n, scatter, after = stages[s]
        base, mine = base_of(s), rank(group)
        for d in range(1, n):
            to = lax.rem(mine + d, n)
            start = pl.multiple_of(base + (to * after if scatter else 0), 8)
            slot = d - 1 if scatter else mine
            yield pltpu.make_async_remote_copy(
                src_ref=acc.at[q, pl.ds(start, after)], dst_ref=stage_bufs[s].at[q, slot],
                send_sem=rs_send.at[q, s, d], recv_sem=rs_recv.at[q, s, d],
                device_id=member(group, d), device_id_type=MESH,
            )

    def rs_start(q, s):
        for c in rs_copies(q, s):
            c.start()

    def rs_end(q, s):
        group, n, scatter, after = stages[s]
        start = pl.multiple_of(base_of(s + 1), 8)
        place = pl.ds(start, after)
        buf = stage_bufs[s]
        if not scatter:
            buf[q, rank(group)] = acc[q, place]
        for c in rs_copies(q, s):
            c.wait()
        total = acc[q, place] if scatter else buf[q, 0]
        for j in range(0 if scatter else 1, n - 1 if scatter else n):
            total = total + buf[q, j]
        if s == len(stages) - 1:
            gat[q, place] = total
        else:
            acc[q, place] = total

    def ag_copies(q, s):
        group, n, scatter, after = stages[s]
        place = pl.ds(pl.multiple_of(base_of(s + 1), 8), after)
        for d in range(1, n if scatter else 1):
            yield pltpu.make_async_remote_copy(
                src_ref=gat.at[q, place], dst_ref=gat.at[q, place],
                send_sem=ag_send.at[q, s, d], recv_sem=ag_recv.at[q, s, d],
                device_id=member(group, d), device_id_type=MESH,
            )

    def ag_start(q, s):
        for c in ag_copies(q, s):
            c.start()

    def ag_end(q, s):
        for c in ag_copies(q, s):
            c.wait()

    def sum_steps():
        steps = []
        last = len(stages) - 1
        for s in range(last + 1):
            steps.append((lambda i, s=s: rs_start(i, s), lambda i, s=s: rs_end(i, s)))
        for s in range(last, -1, -1):
            steps.append((lambda i, s=s: ag_start(i, s), lambda i, s=s: ag_end(i, s)))
        return steps

    running = []

    def advance():
        for part, steps in list(running):
            steps.pop(0)[1](part)
            if steps:
                steps[0][0](part)
            else:
                running.remove((part, steps))

    def begin(part):
        steps = sum_steps()
        steps[0][0](part)
        running.append((part, steps))

    for f in range(4):
        grad[0, f, :OVL] = jnp.zeros((OVL, w), F32)
        grad[0, f, OVL + w :] = jnp.zeros((OVL, w), F32)
    for f in range(4, 6):
        grad[0, f] = jnp.zeros((full, w), F32)
    loads[0].wait()
    pl.semaphore_wait(barrier, expected)
    send(0, 0)
    send(0, 1)
    for load in loads[1:]:
        load.wait()
    kern_ref[0] = jnp.cos(phase_ref[...])
    kern_ref[1] = jnp.sin(phase_ref[...])
    ziel[...] = jnp.zeros_like(ziel)
    receive(0, 1.0, 0)
    receive(0, 1.0, 1)

    half = 1
    parts = modes // half

    def sum_at(q, m, k):
        return q * parts + m // half, (m % half * 2 + k) * w

    rate = PROBE_RATE / math.sqrt(n_row * n_col)
    kern = (kern_ref[0], kern_ref[1])
    conj_kern = (kern[0], -kern[1])
    tables = ((tab_ref[0], tab_ref[1]), (tab_ref[2], tab_ref[3]))
    lane_w = lax.broadcasted_iota(jnp.int32, (w, w), 1)

    for b in range(batches):
        if b == 0 or b == 1:
            source = probe_ref
        else:
            while running:
                advance()
            previous = probe_ref if b == 2 else pnow
            for m in range(modes):
                for k in range(2):
                    i, at = sum_at(b - 2, m, k)
                    pnow[m, k] = previous[m, k] - rate * gat[i, at : at + w]
            source = pnow
        y0, x0 = off_ref[b, 0], off_ref[b, 1]
        start = x0 - OVL
        back = lax.rem(w - start, w)
        back_half = lax.rem(w + w // 2 - start, w)
        inside = (lane_w + start >= 0) & (lane_w + start < w)

        def window(f):
            main = ext[f, pl.ds(y0, w), :]
            side = ext[4 + f // 2, pl.ds(y0, w), :]
            return jnp.where(
                inside,
                pltpu.roll(main, back, 1),
                pltpu.roll(side, back_half if f % 2 else back, 1),
            )

        o1, o2 = (window(0), window(1)), (window(2), window(3))
        probe = [(source[m, 0], source[m, 1]) for m in range(modes)]
        spectrum = dft([cmul(p, o1) for p in probe], tables, False)
        phi = dft([cmul(v, kern) for v in spectrum], tables, True)
        for m in range(modes):
            phi_ref[m, 0], phi_ref[m, 1] = phi[m]
        advance()
        far = dft([cmul(v, o2) for v in phi], tables, False)
        intensity = far[0][0] * far[0][0] + far[0][1] * far[0][1]
        for v in far[1:]:
            intensity = intensity + (v[0] * v[0] + v[1] * v[1])
        factor = 1.0 - amp_ref[b] / jnp.sqrt(intensity + FLOOR)
        chi2 = dft([(v[0] * factor, v[1] * factor) for v in far], tables, True)
        advance()
        g2 = csum([conj_mul((phi_ref[m, 0], phi_ref[m, 1]), chi2[m]) for m in range(modes)])
        ahead = lax.rem(w + start, w)
        outside = (lane - start < 0) | (lane - start >= w)

        def place(p, pair):
            others = []
            for f in (2 * p, 2 * p + 1):
                ziel[f, 2 * OVL : 2 * OVL + w] = pair[f % 2]
                moved = pltpu.roll(ziel[f, pl.ds(2 * OVL - y0, full), :], ahead, 1)
                grad[b + 1, f] = jnp.where(row_ok & jnp.logical_not(outside), moved, 0.0)
                others.append(jnp.where(outside, moved, 0.0))
            grad[b + 1, 4 + p] = jnp.where(side_ok, others[0] + swap(others[1]), 0.0)
            send(b + 1, p)

        place(1, g2)
        q = min(b, max(batches - 2, 0))
        final = b == batches - 1
        starts_sum = b != batches - 2 or batches == 1
        g1 = None

        def keep(group, chi1):
            for m, v in zip(group, chi1):
                g = conj_mul(o1, v)
                for k in range(2):
                    i, at = sum_at(q, m, k)
                    place_at = pl.ds(at, w)
                    acc[i, place_at] = g[k] if b == q else acc[i, place_at] + g[k]

        kept = []
        step = 2 if final and modes % 2 == 0 else modes
        for first in range(0, modes, step):
            group = range(first, first + step)
            spectrum = dft([conj_mul(o2, chi2[m]) for m in group], tables, False)
            chi1 = dft([cmul(v, conj_kern) for v in spectrum], tables, True)
            if final:
                keep(group, chi1)
                if first:
                    advance()
                for part in range(first // half, (first + step) // half):
                    begin(q * parts + part)
            else:
                kept.append((group, chi1))
            term = csum(
                [conj_mul((source[m, 0], source[m, 1]), v) for m, v in zip(group, chi1)]
            )
            g1 = term if g1 is None else csum([g1, term])
        if not final:
            advance()
        place(0, g1)
        advance()
        for group, chi1 in kept:
            keep(group, chi1)
        if starts_sum and not final:
            while running:
                advance()
            for part in range(parts):
                begin(q * parts + part)
        receive(b + 1, -OBJECT_RATE, 1)
        if final:
            advance()
        receive(b + 1, -OBJECT_RATE, 0)
        advance()
        if final:
            for f in range(4):
                obj_out[f] = ext[f, OVL : OVL + w]

    while running:
        advance()
    q = max(batches - 2, 0)
    last = pnow if batches > 2 else probe_ref
    for m in range(modes):
        for k in range(2):
            i, at = sum_at(q, m, k)
            probe_out[m, k] = last[m, k] - rate * gat[i, at : at + w]
    for e in range(batches + 1):
        sent(e)


def per_device(n_row, n_col, object_field, probe, kernel_phase, amplitudes, offsets):
    batches = amplitudes.shape[0]
    modes, _, w, _ = probe.shape
    full = w + 2 * OVL
    parts = modes
    rows = modes * 2 * w // parts
    stages = stages_of(rows, n_row, n_col)
    sums = max(batches - 1, 1) * parts
    most = max(n for _, n, _, _ in stages)
    vmem, smem = pltpu.VMEM, pltpu.SMEM
    dma = pltpu.SemaphoreType.DMA
    scratch = [
        vmem((6, full, w), F32),
        vmem((4, full + 2 * OVL, w), F32),
        vmem((batches + 1, 6, full, w), F32),
        vmem((batches + 1, 2, 2, full, w), F32),
        vmem((batches + 1, 2, 6, 2 * OVL, w), F32),
        vmem((batches + 1, 2, 2, full, w), F32),
        vmem((batches + 1, 4, 2, 2 * OVL, w), F32),
        vmem((modes, 2, w, w), F32),
        vmem((2, w, w), F32),
        vmem((modes, 2, w, w), F32),
        vmem((sums, rows, w), F32),
        vmem((sums, rows, w), F32),
        vmem(probe.shape, F32),
        vmem((w, w), F32),
        vmem((batches, w, w), F32),
        vmem((4, 2 * w, 2 * w), BF16),
    ]
    for _, n, scatter, after in stages:
        scratch.append(vmem((sums, n - 1 if scatter else n, after, w), F32))
    scratch += [dma((5,))] + [dma((batches + 1, 8, 4))] * 2 + [dma((sums, len(stages), most))] * 4
    whole = pl.BlockSpec(memory_space=vmem)
    obj, new_probe = pl.pallas_call(
        functools.partial(kernel, n_row, n_col, batches, modes, stages),
        out_shape=(
            jax.ShapeDtypeStruct((4, w, w), F32),
            jax.ShapeDtypeStruct(probe.shape, F32),
        ),
        in_specs=[pl.BlockSpec(memory_space=smem)] + [pl.BlockSpec(memory_space=pltpu.HBM)] * 5,
        out_specs=(whole, whole),
        scratch_shapes=scratch,
        compiler_params=pltpu.CompilerParams(
            collective_id=0, has_side_effects=True, vmem_limit_bytes=64 * 2**20 - 64 * 2**10
        ),
    )(
        offsets.reshape(batches, 2),
        object_field.reshape(4, w, w),
        probe,
        kernel_phase,
        amplitudes.reshape(batches, w, w),
        jnp.asarray(dft_matrices(w)),
    )
    return obj.reshape(object_field.shape), new_probe


def solution(mesh):
    in_specs = (
        P(None, None, "row", "col"),
        P(),
        P(),
        P(None, "row", "col", None, None),
        P(None, "row", "col", None),
    )
    out_specs = (P(None, None, "row", "col"), P())
    return jax.shard_map(
        functools.partial(per_device, mesh.shape["row"], mesh.shape["col"]),
        mesh=mesh, in_specs=in_specs, out_specs=out_specs, check_vma=False,
    )
```
